32 devices in a mesh: slab: 4 (over y, x), kmom: 4 (over z), energy: 2 (over core).
Axes of the slice: x: 2, y: 2, z: 4, core: 2. Of those that a mesh axis runs over, the one named last changes fastest.
Arguments:
- free_green: float32 [4, 2, 4, 2, 256, 256], P('slab', 'energy', 'kmom'), as said below
- coupling: float32 [4, 256, 256], P('slab'), may hold values from -0.375 to 0.375
- coupling_tiles: int32 [4, 8, 3], P('slab'), may hold values from 0 to 7, as said below
- occupation: float32 [2], P('energy'), may hold values from 0.05 to 1
- phonon_weight: float32 [2, 4, 4], replicated, may hold values from 0.2 to 1
- phonon_mode: int32 [2], replicated, may hold values from 0 to 1, each once
Outputs:
- green: float32 [4, 2, 4, 2, 256, 256], P('slab', 'energy', 'kmom')
- self_energy: bfloat16 [4, 2, 4, 2, 256, 256], P('slab', 'energy', 'kmom')
The draws below stay inside these ranges and needn't reach their ends.
Inputs may be any that keep to these rules, and one draw needn't show every extreme that they name: `coupling_tiles`: the 3 column tiles of one row tile are distinct. `phonon_mode`: each value once. `free_green`: the imaginary part of every diagonal entry is negative.
All inputs are finite; a program needn't handle non-finite values.
Results may differ from the reference program's by a relative error of at most 0.0034.
Values may be sent and summed in bfloat16 or wider, within the bound.
A program may use at most 64 MiB of HBM per device.

```python
import math
import jax
import jax.numpy as jnp
from jax import lax

NB = 256
NTILE = 8
NNZ = 3
BRANCHES = 2
NSLAB = 4
ENERGIES = 2
MOMENTA = 4


def draw_free_green(key, part):
    key_sym, key_anti, key_common, key_diag = jax.random.split(key, 4)
    shape = (NSLAB, ENERGIES, MOMENTA, 2, NB, NB)
    anti_shape = (NSLAB, ENERGIES, MOMENTA, NB, NB)
    common_shape = (NSLAB, 1, 1, NB, NB)
    sym_noise = jax.random.normal(key_sym, shape, jnp.float32)
    anti_noise = jax.random.normal(key_anti, anti_shape, jnp.float32)
    common_noise = jax.random.normal(key_common, common_shape, jnp.float32)
    scale = 1.0 / jnp.sqrt(2.0 * NB)
    symmetric = 0.3 * (sym_noise + jnp.swapaxes(sym_noise, -1, -2)) * scale
    anti_own = anti_noise - jnp.swapaxes(anti_noise, -1, -2)
    anti_common = common_noise - jnp.swapaxes(common_noise, -1, -2)
    anti_real = 0.6 * (anti_own + anti_common) * scale
    antisymmetric = jnp.stack([anti_real, jnp.zeros_like(anti_real)], axis=3)
    diag_draw = jax.random.uniform(key_diag, (NSLAB, ENERGIES, MOMENTA, 2, NB), jnp.float32)
    diag_real = 2.0 * diag_draw[:, :, :, 0, :] - 1.0
    diag_imag = -(0.3 + 1.2 * diag_draw[:, :, :, 1, :])
    diagonal = jnp.stack([diag_real, diag_imag], axis=3)
    identity = jnp.eye(NB, dtype=jnp.float32)
    return symmetric + antisymmetric + diagonal[..., None] * identity


def draw_coupling_tiles(key, part):
    keys = jax.random.split(key, NSLAB * NTILE)
    picked = jax.vmap(lambda single: jax.random.permutation(single, NTILE)[:NNZ])(keys)
    return picked.reshape(NSLAB, NTILE, NNZ).astype(jnp.int32)


def steps_of(own_key, shape, pieces, low, top_value):
    gain, own = 1.0, jax.random.fold_in(own_key, 6)
    for dim, blocks in pieces:
        steps = jnp.exp(jax.random.uniform(jax.random.fold_in(own, dim), (blocks,), jnp.float32, low / len(pieces), top_value / len(pieces)))
        gain = gain * jnp.repeat(steps, shape[dim] // blocks).reshape([-1 if axis == dim else 1 for axis in range(len(shape))])
    return gain


def centred(rng, shape, spread, limit, pieces=(), kind=jnp.bfloat16):
    array = jax.random.normal(rng, shape, jnp.float32) * spread
    if len(pieces) > 0:
        array = steps_of(rng, shape, pieces, -0.22, 0.18) * array
    return jnp.clip(array, min=-limit, max=limit).astype(kind)


def setup_inputs(seed: int = 0) -> dict:
    key_of = jax.random.split(jax.random.key(seed), 7)
    return {
        "free_green": draw_free_green(jax.random.fold_in(key_of[6], 71), 0),
        "coupling": centred(key_of[1], (NSLAB, NB, NB), NB ** -0.5, 0.375, ((0, 4),), jnp.float32),
        "coupling_tiles": draw_coupling_tiles(jax.random.fold_in(key_of[6], 71), 0),
        "occupation": jnp.clip(0.05 + 0.95 * jax.random.uniform(key_of[3], (ENERGIES,), jnp.float32) ** steps_of(key_of[3], (ENERGIES,), ((0, 2),), -0.2, 0.2), 0.05, 1.0),
        "phonon_weight": jnp.clip(jnp.exp(jax.random.uniform(key_of[4], (BRANCHES, MOMENTA, MOMENTA), jnp.float32, math.log(0.2), math.log(1.0))), 0.2, 1.0),
        "phonon_mode": jax.random.permutation(key_of[5], BRANCHES).astype(jnp.int32),
    }


def complex_product(left_factor, right_factor):
    left_real = left_factor[..., 0, :, :]
    left_imag = left_factor[..., 1, :, :]
    right_real = right_factor[..., 0, :, :]
    right_imag = right_factor[..., 1, :, :]
    highest = lax.Precision.HIGHEST
    real_part = jnp.matmul(left_real, right_real, precision=highest) - jnp.matmul(left_imag, right_imag, precision=highest)
    imag_part = jnp.matmul(left_real, right_imag, precision=highest) + jnp.matmul(left_imag, right_real, precision=highest)
    return jnp.stack([real_part, imag_part], axis=-3)


def sandwich(pair_map, inner):
    return complex_product(complex_product(pair_map, inner), jnp.swapaxes(pair_map, -1, -2))


def self_energy_of(green_blocks, occupation, phonon_weight, shifts):
    filling = occupation[:, None, None, None]
    real_part = -filling * (green_blocks[:, :, 0] - jnp.swapaxes(green_blocks[:, :, 0], -1, -2))
    imag_part = -filling * (green_blocks[:, :, 1] + jnp.swapaxes(green_blocks[:, :, 1], -1, -2))
    lesser = jnp.stack([real_part, imag_part], axis=2).astype(jnp.bfloat16)
    lesser = lax.optimization_barrier(lesser).astype(jnp.float32)
    padded = jnp.pad(lesser, ((1, 1), (0, 0), (0, 0), (0, 0), (0, 0)))
    summed = jnp.zeros(lesser.shape, jnp.float32)
    for branch in range(BRANCHES):
        shift_now = shifts[branch]
        upper_slice = lax.dynamic_slice_in_dim(padded, 1 + shift_now, ENERGIES, 0)
        lower_slice = lax.dynamic_slice_in_dim(padded, 1 - shift_now, ENERGIES, 0)
        summed = summed + jnp.einsum('kq,eqcij->ekcij', phonon_weight[branch], upper_slice + lower_slice, precision=lax.Precision.HIGHEST)
    return summed.astype(jnp.bfloat16)


def reference(free_green, coupling, coupling_tiles, occupation, phonon_weight, phonon_mode):
    tile_size = NB // NTILE
    column_tile = jnp.arange(NB, dtype=jnp.int32) // tile_size
    tile_hit = jnp.any(coupling_tiles[..., None] == column_tile, axis=-2).astype(jnp.float32)
    tile_mask = jnp.repeat(tile_hit, tile_size, axis=1)
    coupled = coupling * tile_mask
    shifts = phonon_mode.astype(jnp.int32)
    beyond = jnp.zeros(free_green.shape[1:], jnp.float32)
    greens = []
    selfs = []
    for index in range(NSLAB - 1, -1, -1):
        pair_map = jnp.einsum('ekcij,jl->ekcil', free_green[index], coupled[index], precision=lax.Precision.HIGHEST)
        beyond = free_green[index] + sandwich(pair_map, beyond)
        greens.append(beyond)
        selfs.append(self_energy_of(beyond, occupation, phonon_weight, shifts))
    return jnp.stack(greens[::-1]), jnp.stack(selfs[::-1])
```

```python
import functools

import jax
import jax.numpy as jnp
from jax import lax
from jax.experimental import pallas as pl
from jax.experimental.pallas import tpu as pltpu
from jax.sharding import PartitionSpec as P

F32 = jnp.float32
BF16 = jnp.bfloat16
CHUNKS = 2


def mm(a, b):
    return jnp.dot(a, b, preferred_element_type=F32)


def split(x):
    high = x.astype(BF16)
    return high, (x - high.astype(F32)).astype(BF16)


def fold(products, nb):
    return (
        products[:nb, :nb] - products[nb:, nb:],
        products[:nb, nb:] + products[nb:, :nb],
    )


def remote(src, dst, send_sem, recv_sem, **where):
    return pltpu.make_async_remote_copy(
        src_ref=src,
        dst_ref=dst,
        send_sem=send_sem,
        recv_sem=recv_sem,
        device_id=where,
        device_id_type=pl.DeviceIdType.MESH,
    )


def kernel(
    sizes, g_hbm, c_hbm, tiles, occ, weight, mode, green_hbm, self_hbm,
    a_ref, c_ref, qh, ql, qth, qtl, send_a, send_q, got_a, got_q,
    packed, sum0, sum1, near, out_ref,
    in_sem, out_sem, sa_sem, sq_sem, ra_sem, rq_sem,
    right_sem, left_sem, block_sem, es_sem, er_sem,
):
    slabs, momenta, energies, levels = sizes
    nb = c_ref.shape[0]
    j = lax.axis_index("slab")
    k = lax.axis_index("kmom")
    e = lax.axis_index("energy")

    load_g = pltpu.make_async_copy(g_hbm, a_ref, in_sem.at[0])
    load_c = pltpu.make_async_copy(c_hbm, c_ref, in_sem.at[1])
    load_g.start()
    load_c.start()

    barrier = pltpu.get_barrier_semaphore()

    def greet(**where):
        pl.semaphore_signal(
            barrier, inc=1, device_id=where, device_id_type=pl.DeviceIdType.MESH
        )

    for step in range(1, slabs):
        greet(slab=lax.rem(j + step, slabs))
    pl.when(k > 0)(lambda: greet(kmom=k - 1))
    pl.when(k < momenta - 1)(lambda: greet(kmom=k + 1))
    pl.when(e > 0)(lambda: greet(energy=e - 1))
    pl.when(e < energies - 1)(lambda: greet(energy=e + 1))

    load_g.wait()

    def pack_for_send(buffer):
        buffer[:, :nb] = a_ref[:nb, :].astype(BF16)
        buffer[:, nb:] = a_ref[nb:, :].astype(BF16)

    peers = slabs - 1
    for there in (k > 0, k < momenta - 1, e > 0, e < energies - 1):
        peers += jnp.where(there, 1, 0)
    pl.semaphore_wait(barrier, peers)

    def a_copy(level, to):
        return remote(
            send_a, got_a.at[level], sa_sem.at[to], ra_sem.at[level],
            slab=lax.max(j - 1 - to, 0),
        )

    def q_copy(level, to):
        return remote(
            send_q, got_q.at[level], sq_sem.at[to], rq_sem.at[level],
            slab=lax.max(j - 1 - to, 0),
        )

    def roles(level):
        half = 1 << level
        base = (j // (2 * half)) * (2 * half)
        sender = lax.rem(j, 2 * half) == half
        receiver = jnp.logical_and(lax.rem(j, 2 * half) < half, base + half < slabs)
        with_q = base + 2 * half < slabs
        return half, sender, receiver, with_q

    def send_own_a(level):
        pack_for_send(send_a)
        for to in range(1 << level):
            a_copy(level, to).start()

    pl.when(roles(0)[1])(lambda: send_own_a(0))

    load_c.wait()

    def set_q(q):
        high, low = split(q)
        qh[...] = high
        ql[...] = low
        high, low = split(q.T)
        qth[...] = high
        qtl[...] = low

    @pl.when(j < slabs - 1)
    def _():
        gh, gl = split(a_ref[...])
        size = nb // tiles.shape[1]
        parts = []
        column = lax.broadcasted_iota(jnp.int32, (size, nb), 1) // size
        for row in range(tiles.shape[1]):
            hit = column == tiles[0, row, 0]
            for other in range(1, tiles.shape[2]):
                hit = jnp.logical_or(hit, column == tiles[0, row, other])
            rows = pl.ds(row * size, size)
            parts.append(jnp.where(hit, c_ref[rows, :], 0.0))
        ch, cl = split(jnp.concatenate(parts, axis=0))
        set_q(mm(gh, ch) + mm(gl, ch) + mm(gh, cl))

    for level in range(levels):
        half, sender, receiver, with_q = roles(level)

        @pl.when(sender)
        def _():
            if level > 0:
                send_own_a(level)

            @pl.when(with_q)
            def _():
                send_q[:, :nb] = qh[:nb, :]
                send_q[:, nb:] = qh[nb:, :]
                for to in range(half):
                    q_copy(level, to).start()

        @pl.when(receiver)
        def _():
            a_copy(level, 0).wait_recv()
            beyond = got_a[level]
            t_real, t_imag = fold(mm(qh[...], beyond) + mm(ql[...], beyond), nb)
            th, tl = split(jnp.concatenate([t_real, t_imag], axis=0))
            real, imag = fold(mm(th, qth[...]) + mm(tl, qth[...]) + mm(th, qtl[...]), nb)
            a_ref[:nb, :] += real
            a_ref[nb:, :] += imag

            @pl.when(with_q)
            def _():
                q_copy(level, 0).wait_recv()
                later = got_q[level]
                q_real, q_imag = fold(mm(qh[...], later) + mm(ql[...], later), nb)
                set_q(jnp.concatenate([q_real, q_imag], axis=0))

    store_green = pltpu.make_async_copy(a_ref, green_hbm, out_sem.at[0])
    store_green.start()

    row = lax.broadcasted_iota(jnp.int32, (nb, nb), 0)
    col = lax.broadcasted_iota(jnp.int32, (nb, nb), 1)
    real, imag = a_ref[:nb, :], a_ref[nb:, :]
    mirrored = jnp.where(col < row, -real, imag).T
    packed[k] = (-occ[0] * (jnp.where(col > row, real, imag) + mirrored)).astype(BF16)

    rows_of = [pl.ds(c * (nb // CHUNKS), nb // CHUNKS) for c in range(CHUNKS)]

    def to_right(q, c):
        block = packed.at[q, rows_of[c]]
        return remote(
            block, block, right_sem.at[q, c], block_sem.at[q, c],
            kmom=lax.min(k + 1, momenta - 1),
        )

    def to_left(q, c):
        block = packed.at[q, rows_of[c]]
        return remote(
            block, block, left_sem.at[q, c], block_sem.at[q, c], kmom=lax.max(k - 1, 0)
        )

    def near_copy(side, c):
        target = lax.min(e + 1, energies - 1) if side == 0 else lax.max(e - 1, 0)
        return remote(
            sum1.at[rows_of[c]], near.at[side, rows_of[c]],
            es_sem.at[side, c], er_sem.at[side, c], energy=target,
        )

    has_right, has_left = k < momenta - 1, k > 0
    has_next, has_before = e < energies - 1, e > 0

    for c in range(CHUNKS):
        pl.when(has_right)(lambda: to_right(k, c).start())
        pl.when(has_left)(lambda: to_left(k, c).start())

    def weights(q):
        w0, w1 = jnp.float32(0), jnp.float32(0)
        for branch in range(weight.shape[0]):
            value = weight[branch, k, q]
            w0 += jnp.where(mode[branch] == 0, 2.0 * value, 0.0)
            w1 += jnp.where(mode[branch] == 0, 0.0, value)
        return w0, w1

    own0, own1 = weights(k)
    for c in range(CHUNKS):
        block = packed[k, rows_of[c]].astype(F32)
        sum0[rows_of[c]] = own0 * block
        sum1[rows_of[c]] = own1 * block

    def take(q, c):
        w0, w1 = weights(q)
        block = packed[q, rows_of[c]].astype(F32)
        sum1[rows_of[c]] += w1 * block
        sum0[rows_of[c]] += w0 * block

    for step in range(1, momenta):
        low, high = k - step, k + step
        for c in range(CHUNKS):

            @pl.when(low >= 0)
            def _():
                q = lax.max(low, 0)
                to_right(q, c).wait_recv()
                pl.when(has_right)(lambda: to_right(q, c).start())

            @pl.when(high < momenta)
            def _():
                q = lax.min(high, momenta - 1)
                to_left(q, c).wait_recv()
                pl.when(has_left)(lambda: to_left(q, c).start())

            pl.when(low >= 0)(lambda: take(lax.max(low, 0), c))
            pl.when(high < momenta)(lambda: take(lax.min(high, momenta - 1), c))
            if step == momenta - 1:
                pl.when(has_next)(lambda: near_copy(0, c).start())
                pl.when(has_before)(lambda: near_copy(1, c).start())
    if momenta == 1:
        for c in range(CHUNKS):
            pl.when(has_next)(lambda: near_copy(0, c).start())
            pl.when(has_before)(lambda: near_copy(1, c).start())

    for c in range(CHUNKS):

        @pl.when(has_before)
        def _():
            near_copy(0, c).wait_recv()
            sum0[rows_of[c]] += near[0, rows_of[c]]

        @pl.when(has_next)
        def _():
            near_copy(1, c).wait_recv()
            sum0[rows_of[c]] += near[1, rows_of[c]]

    total = sum0[...]
    turned = total.T
    out_ref[:nb, :] = jnp.where(
        col > row, total, jnp.where(col < row, -turned, 0.0)
    ).astype(BF16)
    out_ref[nb:, :] = jnp.where(row >= col, total, turned).astype(BF16)
    store_self = pltpu.make_async_copy(out_ref, self_hbm, out_sem.at[1])
    store_self.start()

    for level in range(levels):
        half, sender, receiver, with_q = roles(level)

        @pl.when(sender)
        def _():
            for to in range(half):
                a_copy(level, to).wait_send()

            @pl.when(with_q)
            def _():
                for to in range(half):
                    q_copy(level, to).wait_send()

    for c in range(CHUNKS):
        for q in range(momenta):
            pl.when(jnp.logical_and(has_right, q <= k))(
                lambda: to_right(q, c).wait_send()
            )
            pl.when(jnp.logical_and(has_left, q >= k))(lambda: to_left(q, c).wait_send())
        pl.when(has_next)(lambda: near_copy(0, c).wait_send())
        pl.when(has_before)(lambda: near_copy(1, c).wait_send())
    store_green.wait()
    store_self.wait()


def on_device(free_green, coupling, coupling_tiles, occupation, phonon_weight, phonon_mode):
    slabs = lax.axis_size("slab")
    momenta = lax.axis_size("kmom")
    energies = lax.axis_size("energy")
    nb = coupling.shape[-1]
    levels = max((slabs - 1).bit_length(), 1)
    most = 1 << (levels - 1)
    smem = pl.BlockSpec(memory_space=pltpu.SMEM)
    hbm = pl.BlockSpec(memory_space=pltpu.HBM)
    dma = pltpu.SemaphoreType.DMA
    green, self_energy = pl.pallas_call(
        functools.partial(kernel, (slabs, momenta, energies, levels)),
        out_shape=(
            jax.ShapeDtypeStruct((2 * nb, nb), F32),
            jax.ShapeDtypeStruct((2 * nb, nb), BF16),
        ),
        in_specs=[hbm, hbm, smem, smem, smem, smem],
        out_specs=(hbm, hbm),
        scratch_shapes=[
            pltpu.VMEM((2 * nb, nb), F32),
            pltpu.VMEM((nb, nb), F32),
            pltpu.VMEM((2 * nb, nb), BF16),
            pltpu.VMEM((2 * nb, nb), BF16),
            pltpu.VMEM((nb, 2 * nb), BF16),
            pltpu.VMEM((nb, 2 * nb), BF16),
            pltpu.VMEM((nb, 2 * nb), BF16),
            pltpu.VMEM((nb, 2 * nb), BF16),
            pltpu.VMEM((levels, nb, 2 * nb), BF16),
            pltpu.VMEM((levels, nb, 2 * nb), BF16),
            pltpu.VMEM((momenta, nb, nb), BF16),
            pltpu.VMEM((nb, nb), F32),
            pltpu.VMEM((nb, nb), F32),
            pltpu.VMEM((2, nb, nb), F32),
            pltpu.VMEM((2 * nb, nb), BF16),
            dma((2,)),
            dma((2,)),
            dma((most,)),
            dma((most,)),
            dma((levels,)),
            dma((levels,)),
            dma((momenta, CHUNKS)),
            dma((momenta, CHUNKS)),
            dma((momenta, CHUNKS)),
            dma((2, CHUNKS)),
            dma((2, CHUNKS)),
        ],
        compiler_params=pltpu.CompilerParams(
            collective_id=0, has_side_effects=True, vmem_limit_bytes=40 * 1024 * 1024
        ),
    )(
        free_green.reshape(2 * nb, nb),
        coupling.reshape(nb, nb),
        coupling_tiles,
        occupation,
        phonon_weight,
        phonon_mode,
    )
    return green.reshape(free_green.shape), self_energy.reshape(free_green.shape)


def solution(mesh):
    in_specs = (
        P("slab", "energy", "kmom", None, None, None),
        P("slab", None, None),
        P("slab", None, None),
        P("energy"),
        P(),
        P(),
    )
    out_specs = (
        P("slab", "energy", "kmom", None, None, None),
        P("slab", "energy", "kmom", None, None, None),
    )
    return jax.shard_map(
        on_device, mesh=mesh, in_specs=in_specs, out_specs=out_specs, check_vma=False
    )
```

```python
import functools

import jax
import jax.numpy as jnp
from jax import lax
from jax.experimental import pallas as pl
from jax.experimental.pallas import tpu as pltpu
from jax.sharding import PartitionSpec as P

F32 = jnp.float32
BF16 = jnp.bfloat16
CHUNKS = 2
VMEM_BYTES = 62 * 1024 * 1024


def mm(a, b):
    return jnp.dot(a, b, preferred_element_type=F32)


def split(x):
    high = x.astype(BF16)
    return high, (x - high.astype(F32)).astype(BF16)


def fold(products, nb):
    return (
        products[:nb, :nb] - products[nb:, nb:],
        products[:nb, nb:] + products[nb:, :nb],
    )


def remote(src, dst, send_sem, recv_sem, **where):
    return pltpu.make_async_remote_copy(
        src_ref=src,
        dst_ref=dst,
        send_sem=send_sem,
        recv_sem=recv_sem,
        device_id=where,
        device_id_type=pl.DeviceIdType.MESH,
    )


def kernel(
    sizes, g_hbm, c_hbm, tiles_hbm, occ_hbm, weight_hbm, mode_hbm, green_hbm, self_hbm,
    tiles, occ, weight, mode, a_ref, c_ref, qh, ql, qth, qtl, send_a, send_q, got_a, got_q,
    packed, sum0, sum1, near, out_ref,
    in_sem, out_sem, sa_sem, sq_sem, ra_sem, rq_sem,
    right_sem, left_sem, block_sem, es_sem, er_sem,
):
    slabs, momenta, energies, levels = sizes
    nb = c_ref.shape[0]
    j = lax.axis_index("slab")
    k = lax.axis_index("kmom")
    e = lax.axis_index("energy")

    load_g = pltpu.make_async_copy(g_hbm, a_ref, in_sem.at[0])
    load_c = pltpu.make_async_copy(c_hbm, c_ref, in_sem.at[1])
    load_g.start()
    load_c.start()
    small_loads = [
        pltpu.make_async_copy(source, target, in_sem.at[2 + index])
        for index, (source, target) in enumerate(
            ((tiles_hbm, tiles), (occ_hbm, occ), (weight_hbm, weight), (mode_hbm, mode))
        )
    ]
    for load in small_loads:
        load.start()

    barrier = pltpu.get_barrier_semaphore()

    def greet(**where):
        pl.semaphore_signal(
            barrier, inc=1, device_id=where, device_id_type=pl.DeviceIdType.MESH
        )

    for step in range(1, slabs):
        greet(slab=lax.rem(j + step, slabs))
    pl.when(k > 0)(lambda: greet(kmom=k - 1))
    pl.when(k < momenta - 1)(lambda: greet(kmom=k + 1))
    pl.when(e > 0)(lambda: greet(energy=e - 1))
    pl.when(e < energies - 1)(lambda: greet(energy=e + 1))

    load_g.wait()

    rows_of = [pl.ds(c * (nb // CHUNKS), nb // CHUNKS) for c in range(CHUNKS)]
    imag_rows_of = [pl.ds(nb + c * (nb // CHUNKS), nb // CHUNKS) for c in range(CHUNKS)]

    peers = slabs - 1
    for there in (k > 0, k < momenta - 1, e > 0, e < energies - 1):
        peers += jnp.where(there, 1, 0)
    pl.semaphore_wait(barrier, peers)

    def a_copy(level, to, c):
        return remote(
            send_a.at[rows_of[c]], got_a.at[level, rows_of[c]],
            sa_sem.at[to, c], ra_sem.at[level, c], slab=lax.max(j - 1 - to, 0),
        )

    def q_copy(level, to):
        return remote(
            send_q, got_q.at[level], sq_sem.at[to], rq_sem.at[level],
            slab=lax.max(j - 1 - to, 0),
        )

    def roles(level):
        half = 1 << level
        base = (j // (2 * half)) * (2 * half)
        sender = lax.rem(j, 2 * half) == half
        receiver = jnp.logical_and(lax.rem(j, 2 * half) < half, base + half < slabs)
        with_q = base + 2 * half < slabs
        return half, sender, receiver, with_q

    def send_a_chunk(level, c):
        send_a[rows_of[c], :nb] = a_ref[rows_of[c], :].astype(BF16)
        send_a[rows_of[c], nb:] = a_ref[imag_rows_of[c], :].astype(BF16)
        for to in range(1 << level):
            a_copy(level, to, c).start()

    @pl.when(roles(0)[1])
    def _():
        for c in range(CHUNKS):
            send_a_chunk(0, c)

    load_c.wait()
    for load in small_loads:
        load.wait()

    def set_q(q):
        high, low = split(q)
        qh[...] = high
        ql[...] = low
        high, low = split(q.T)
        qth[...] = high
        qtl[...] = low

    @pl.when(j < slabs - 1)
    def _():
        gh, gl = split(a_ref[...])
        size = nb // tiles.shape[2]
        parts = []
        column = lax.broadcasted_iota(jnp.int32, (size, nb), 1) // size
        for row in range(tiles.shape[2]):
            hit = column == tiles[0, 0, row]
            for other in range(1, tiles.shape[0]):
                hit = jnp.logical_or(hit, column == tiles[other, 0, row])
            rows = pl.ds(row * size, size)
            parts.append(jnp.where(hit, c_ref[rows, :], 0.0))
        ch, cl = split(jnp.concatenate(parts, axis=0))
        set_q(mm(gh, ch) + mm(gl, ch) + mm(gh, cl))

    for level in range(levels):
        half, sender, receiver, with_q = roles(level)

        @pl.when(sender)
        def _():
            @pl.when(with_q)
            def _():
                send_q[:, :nb] = qh[:nb, :]
                send_q[:, nb:] = qh[nb:, :]
                for to in range(half):
                    q_copy(level, to).start()

        @pl.when(receiver)
        def _():
            products = jnp.zeros((2 * nb, 2 * nb), F32)
            for c in range(CHUNKS):
                a_copy(level, 0, c).wait_recv()
                beyond = got_a[level, rows_of[c]]
                products += mm(qh[:, rows_of[c]], beyond) + mm(ql[:, rows_of[c]], beyond)
            t_real, t_imag = fold(products, nb)
            rows = nb // CHUNKS
            for c in range(CHUNKS):
                own = slice(c * rows, (c + 1) * rows)
                th, tl = split(jnp.concatenate([t_real[own], t_imag[own]], axis=0))
                last = mm(th, qth[...]) + mm(tl, qth[...]) + mm(th, qtl[...])
                a_ref[rows_of[c], :] += last[:rows, :nb] - last[rows:, nb:]
                a_ref[imag_rows_of[c], :] += last[:rows, nb:] + last[rows:, :nb]
                if level + 1 < levels:
                    pl.when(roles(level + 1)[1])(lambda: send_a_chunk(level + 1, c))

            @pl.when(with_q)
            def _():
                q_copy(level, 0).wait_recv()
                later = got_q[level]
                q_real, q_imag = fold(mm(qh[...], later) + mm(ql[...], later), nb)
                set_q(jnp.concatenate([q_real, q_imag], axis=0))

    store_green = pltpu.make_async_copy(a_ref, green_hbm, out_sem.at[0])
    store_green.start()

    row = lax.broadcasted_iota(jnp.int32, (nb, nb), 0)
    col = lax.broadcasted_iota(jnp.int32, (nb, nb), 1)
    real, imag = a_ref[:nb, :], a_ref[nb:, :]
    mirrored = jnp.where(col < row, -real, imag).T
    packed[k] = (-occ[0] * (jnp.where(col > row, real, imag) + mirrored)).astype(BF16)

    def to_right(q, c):
        block = packed.at[q, rows_of[c]]
        return remote(
            block, block, right_sem.at[q, c], block_sem.at[q, c],
            kmom=lax.min(k + 1, momenta - 1),
        )

    def to_left(q, c):
        block = packed.at[q, rows_of[c]]
        return remote(
            block, block, left_sem.at[q, c], block_sem.at[q, c], kmom=lax.max(k - 1, 0)
        )

    def near_copy(side, c):
        target = lax.min(e + 1, energies - 1) if side == 0 else lax.max(e - 1, 0)
        return remote(
            sum1.at[rows_of[c]], near.at[side, rows_of[c]],
            es_sem.at[side, c], er_sem.at[side, c], energy=target,
        )

    has_right, has_left = k < momenta - 1, k > 0
    has_next, has_before = e < energies - 1, e > 0

    for c in range(CHUNKS):
        pl.when(has_right)(lambda: to_right(k, c).start())
        pl.when(has_left)(lambda: to_left(k, c).start())

    def weights(q):
        w0, w1 = jnp.float32(0), jnp.float32(0)
        for branch in range(weight.shape[0]):
            value = weight[branch, k, q]
            w0 += jnp.where(mode[branch] == 0, 2.0 * value, 0.0)
            w1 += jnp.where(mode[branch] == 0, 0.0, value)
        return w0, w1

    own0, own1 = weights(k)
    for c in range(CHUNKS):
        block = packed[k, rows_of[c]].astype(F32)
        sum0[rows_of[c]] = own0 * block
        sum1[rows_of[c]] = own1 * block

    def take(q, c):
        w0, w1 = weights(q)
        block = packed[q, rows_of[c]].astype(F32)
        sum1[rows_of[c]] += w1 * block
        sum0[rows_of[c]] += w0 * block

    for step in range(1, momenta):
        low, high = k - step, k + step
        for c in range(CHUNKS):

            @pl.when(low >= 0)
            def _():
                q = lax.max(low, 0)
                to_right(q, c).wait_recv()
                pl.when(has_right)(lambda: to_right(q, c).start())

            @pl.when(high < momenta)
            def _():
                q = lax.min(high, momenta - 1)
                to_left(q, c).wait_recv()
                pl.when(has_left)(lambda: to_left(q, c).start())

            pl.when(low >= 0)(lambda: take(lax.max(low, 0), c))
            pl.when(high < momenta)(lambda: take(lax.min(high, momenta - 1), c))
            if step == momenta - 1:
                pl.when(has_next)(lambda: near_copy(0, c).start())
                pl.when(has_before)(lambda: near_copy(1, c).start())
    if momenta == 1:
        for c in range(CHUNKS):
            pl.when(has_next)(lambda: near_copy(0, c).start())
            pl.when(has_before)(lambda: near_copy(1, c).start())

    for c in range(CHUNKS):

        @pl.when(has_before)
        def _():
            near_copy(0, c).wait_recv()
            sum0[rows_of[c]] += near[0, rows_of[c]]

        @pl.when(has_next)
        def _():
            near_copy(1, c).wait_recv()
            sum0[rows_of[c]] += near[1, rows_of[c]]

    total = sum0[...]
    turned = total.T
    out_ref[:nb, :] = jnp.where(
        col > row, total, jnp.where(col < row, -turned, 0.0)
    ).astype(BF16)
    out_ref[nb:, :] = jnp.where(row >= col, total, turned).astype(BF16)
    store_self = pltpu.make_async_copy(out_ref, self_hbm, out_sem.at[1])
    store_self.start()

    for level in range(levels):
        half, sender, receiver, with_q = roles(level)

        @pl.when(sender)
        def _():
            for to in range(half):
                for c in range(CHUNKS):
                    a_copy(level, to, c).wait_send()

            @pl.when(with_q)
            def _():
                for to in range(half):
                    q_copy(level, to).wait_send()

    for c in range(CHUNKS):
        for q in range(momenta):
            pl.when(jnp.logical_and(has_right, q <= k))(
                lambda: to_right(q, c).wait_send()
            )
            pl.when(jnp.logical_and(has_left, q >= k))(lambda: to_left(q, c).wait_send())
        pl.when(has_next)(lambda: near_copy(0, c).wait_send())
        pl.when(has_before)(lambda: near_copy(1, c).wait_send())
    store_green.wait()
    store_self.wait()


def on_device(free_green, coupling, coupling_tiles, occupation, phonon_weight, phonon_mode):
    slabs = lax.axis_size("slab")
    momenta = lax.axis_size("kmom")
    energies = lax.axis_size("energy")
    nb = coupling.shape[-1]
    levels = max((slabs - 1).bit_length(), 1)
    most = 1 << (levels - 1)
    hbm = pl.BlockSpec(memory_space=pltpu.HBM)
    dma = pltpu.SemaphoreType.DMA
    green, self_energy = pl.pallas_call(
        functools.partial(kernel, (slabs, momenta, energies, levels)),
        out_shape=(
            jax.ShapeDtypeStruct((2 * nb, nb), F32),
            jax.ShapeDtypeStruct((2 * nb, nb), BF16),
        ),
        in_specs=[hbm] * 6,
        out_specs=(hbm, hbm),
        scratch_shapes=[
            pltpu.SMEM(coupling_tiles.shape[2:] + coupling_tiles.shape[:2], jnp.int32),
            pltpu.SMEM(occupation.shape, F32),
            pltpu.SMEM(phonon_weight.shape, F32),
            pltpu.SMEM(phonon_mode.shape, jnp.int32),
            pltpu.VMEM((2 * nb, nb), F32),
            pltpu.VMEM((nb, nb), F32),
            pltpu.VMEM((2 * nb, nb), BF16),
            pltpu.VMEM((2 * nb, nb), BF16),
            pltpu.VMEM((nb, 2 * nb), BF16),
            pltpu.VMEM((nb, 2 * nb), BF16),
            pltpu.VMEM((nb, 2 * nb), BF16),
            pltpu.VMEM((nb, 2 * nb), BF16),
            pltpu.VMEM((levels, nb, 2 * nb), BF16),
            pltpu.VMEM((levels, nb, 2 * nb), BF16),
            pltpu.VMEM((momenta, nb, nb), BF16),
            pltpu.VMEM((nb, nb), F32),
            pltpu.VMEM((nb, nb), F32),
            pltpu.VMEM((2, nb, nb), F32),
            pltpu.VMEM((2 * nb, nb), BF16),
            dma((6,)),
            dma((2,)),
            dma((most, CHUNKS)),
            dma((most,)),
            dma((levels, CHUNKS)),
            dma((levels,)),
            dma((momenta, CHUNKS)),
            dma((momenta, CHUNKS)),
            dma((momenta, CHUNKS)),
            dma((2, CHUNKS)),
            dma((2, CHUNKS)),
        ],
        compiler_params=pltpu.CompilerParams(
            collective_id=0, has_side_effects=True, vmem_limit_bytes=VMEM_BYTES
        ),
    )(
        free_green.reshape(2 * nb, nb),
        coupling.reshape(nb, nb),
        jnp.transpose(coupling_tiles, (2, 0, 1)),
        occupation,
        phonon_weight,
        phonon_mode,
    )
    return green.reshape(free_green.shape), self_energy.reshape(free_green.shape)


def solution(mesh):
    in_specs = (
        P("slab", "energy", "kmom", None, None, None),
        P("slab", None, None),
        P("slab", None, None),
        P("energy"),
        P(),
        P(),
    )
    out_specs = (
        P("slab", "energy", "kmom", None, None, None),
        P("slab", "energy", "kmom", None, None, None),
    )
    return jax.shard_map(
        on_device, mesh=mesh, in_specs=in_specs, out_specs=out_specs, check_vma=False
    )
```

```python
import functools

import jax
import jax.numpy as jnp
from jax import lax
from jax.experimental import pallas as pl
from jax.experimental.pallas import tpu as pltpu
from jax.sharding import PartitionSpec as P

F32 = jnp.float32
BF16 = jnp.bfloat16
CHUNKS = 2
RELAYS = 4
VMEM_BYTES = 62 * 1024 * 1024


def mm(a, b):
    return jnp.dot(a, b, preferred_element_type=F32)


def split(x):
    high = x.astype(BF16)
    return high, (x - high.astype(F32)).astype(BF16)


def fold(products, nb):
    return (
        products[:nb, :nb] - products[nb:, nb:],
        products[:nb, nb:] + products[nb:, :nb],
    )


def remote(src, dst, send_sem, recv_sem, **where):
    return pltpu.make_async_remote_copy(
        src_ref=src,
        dst_ref=dst,
        send_sem=send_sem,
        recv_sem=recv_sem,
        device_id=where,
        device_id_type=pl.DeviceIdType.MESH,
    )


def kernel(
    sizes, g_hbm, c_hbm, tiles_hbm, occ_hbm, weight_hbm, mode_hbm, green_hbm, self_hbm,
    tiles, occ, weight, mode, a_ref, c_ref, qh, ql, qth, qtl, send_a, send_q, got_a, got_q,
    packed, sum0, sum1, near, out_ref,
    in_sem, out_sem, sa_sem, sq_sem, ra_sem, rq_sem,
    right_sem, left_sem, block_sem, es_sem, er_sem,
):
    slabs, momenta, energies, levels = sizes
    nb = c_ref.shape[0]
    j = lax.axis_index("slab")
    k = lax.axis_index("kmom")
    e = lax.axis_index("energy")

    load_g = pltpu.make_async_copy(g_hbm, a_ref, in_sem.at[0])
    load_c = pltpu.make_async_copy(c_hbm, c_ref, in_sem.at[1])
    load_g.start()
    load_c.start()
    small_loads = [
        pltpu.make_async_copy(source, target, in_sem.at[2 + index])
        for index, (source, target) in enumerate(
            ((tiles_hbm, tiles), (occ_hbm, occ), (weight_hbm, weight), (mode_hbm, mode))
        )
    ]
    for load in small_loads:
        load.start()

    barrier = pltpu.get_barrier_semaphore()

    def greet(**where):
        pl.semaphore_signal(
            barrier, inc=1, device_id=where, device_id_type=pl.DeviceIdType.MESH
        )

    for step in range(1, slabs):
        greet(slab=lax.rem(j + step, slabs))
    pl.when(k > 0)(lambda: greet(kmom=k - 1))
    pl.when(k < momenta - 1)(lambda: greet(kmom=k + 1))
    pl.when(e > 0)(lambda: greet(energy=e - 1))
    pl.when(e < energies - 1)(lambda: greet(energy=e + 1))

    load_g.wait()

    rows_of = [pl.ds(c * (nb // CHUNKS), nb // CHUNKS) for c in range(CHUNKS)]
    imag_rows_of = [pl.ds(nb + c * (nb // CHUNKS), nb // CHUNKS) for c in range(CHUNKS)]

    peers = slabs - 1
    for there in (k > 0, k < momenta - 1, e > 0, e < energies - 1):
        peers += jnp.where(there, 1, 0)
    pl.semaphore_wait(barrier, peers)

    def a_copy(level, to, c):
        return remote(
            send_a.at[rows_of[c]], got_a.at[level, rows_of[c]],
            sa_sem.at[to, c], ra_sem.at[level, c], slab=lax.max(j - 1 - to, 0),
        )

    def q_copy(level, to):
        return remote(
            send_q, got_q.at[level], sq_sem.at[to], rq_sem.at[level],
            slab=lax.max(j - 1 - to, 0),
        )

    def roles(level):
        half = 1 << level
        base = (j // (2 * half)) * (2 * half)
        sender = lax.rem(j, 2 * half) == half
        receiver = jnp.logical_and(lax.rem(j, 2 * half) < half, base + half < slabs)
        with_q = base + 2 * half < slabs
        return half, sender, receiver, with_q

    def send_a_chunk(level, c):
        send_a[rows_of[c], :nb] = a_ref[rows_of[c], :].astype(BF16)
        send_a[rows_of[c], nb:] = a_ref[imag_rows_of[c], :].astype(BF16)
        for to in range(1 << level):
            a_copy(level, to, c).start()

    @pl.when(roles(0)[1])
    def _():
        for c in range(CHUNKS):
            send_a_chunk(0, c)

    load_c.wait()
    for load in small_loads:
        load.wait()

    def set_q(q):
        high, low = split(q)
        qh[...] = high
        ql[...] = low
        high, low = split(q.T)
        qth[...] = high
        qtl[...] = low

    @pl.when(j < slabs - 1)
    def _():
        gh, gl = split(a_ref[...])
        size = nb // tiles.shape[2]
        parts = []
        column = lax.broadcasted_iota(jnp.int32, (size, nb), 1) // size
        for row in range(tiles.shape[2]):
            hit = column == tiles[0, 0, row]
            for other in range(1, tiles.shape[0]):
                hit = jnp.logical_or(hit, column == tiles[other, 0, row])
            rows = pl.ds(row * size, size)
            parts.append(jnp.where(hit, c_ref[rows, :], 0.0))
        ch, cl = split(jnp.concatenate(parts, axis=0))
        set_q(mm(gh, ch) + mm(gl, ch) + mm(gh, cl))

    for level in range(levels):
        half, sender, receiver, with_q = roles(level)

        @pl.when(sender)
        def _():
            @pl.when(with_q)
            def _():
                send_q[:, :nb] = qh[:nb, :]
                send_q[:, nb:] = qh[nb:, :]
                for to in range(half):
                    q_copy(level, to).start()

        @pl.when(receiver)
        def _():
            products = 0.0
            for c in range(CHUNKS):
                a_copy(level, 0, c).wait_recv()
                beyond = got_a[level, rows_of[c]]
                products += mm(
                    jnp.concatenate([qh[:, rows_of[c]], ql[:, rows_of[c]]], axis=1),
                    jnp.concatenate([beyond, beyond], axis=0),
                )
            t_real, t_imag = fold(products, nb)
            rows = nb // CHUNKS
            for c in range(CHUNKS):
                own = slice(c * rows, (c + 1) * rows)
                th, tl = split(jnp.concatenate([t_real[own], t_imag[own]], axis=0))
                last = mm(
                    jnp.concatenate([th, tl, th], axis=1),
                    jnp.concatenate([qth[...], qth[...], qtl[...]], axis=0),
                )
                a_ref[rows_of[c], :] += last[:rows, :nb] - last[rows:, nb:]
                a_ref[imag_rows_of[c], :] += last[:rows, nb:] + last[rows:, :nb]
                if level + 1 < levels:
                    pl.when(roles(level + 1)[1])(lambda: send_a_chunk(level + 1, c))

            @pl.when(with_q)
            def _():
                q_copy(level, 0).wait_recv()
                later = got_q[level]
                q_real, q_imag = fold(mm(qh[...], later) + mm(ql[...], later), nb)
                set_q(jnp.concatenate([q_real, q_imag], axis=0))

    store_green = pltpu.make_async_copy(a_ref, green_hbm, out_sem.at[0])
    store_green.start()

    row = lax.broadcasted_iota(jnp.int32, (nb, nb), 0)
    col = lax.broadcasted_iota(jnp.int32, (nb, nb), 1)
    real, imag = a_ref[:nb, :], a_ref[nb:, :]
    mirrored = jnp.where(col < row, -real, imag).T
    packed[k] = (-occ[0] * (jnp.where(col > row, real, imag) + mirrored)).astype(BF16)

    part_of = [pl.ds(c * (nb // RELAYS), nb // RELAYS) for c in range(RELAYS)]

    def to_right(q, c):
        block = packed.at[q, part_of[c]]
        return remote(
            block, block, right_sem.at[q, c], block_sem.at[q, c],
            kmom=lax.min(k + 1, momenta - 1),
        )

    def to_left(q, c):
        block = packed.at[q, part_of[c]]
        return remote(
            block, block, left_sem.at[q, c], block_sem.at[q, c], kmom=lax.max(k - 1, 0)
        )

    def near_copy(side, c):
        target = lax.min(e + 1, energies - 1) if side == 0 else lax.max(e - 1, 0)
        return remote(
            sum1.at[part_of[c]], near.at[side, part_of[c]],
            es_sem.at[side, c], er_sem.at[side, c], energy=target,
        )

    has_right, has_left = k < momenta - 1, k > 0
    has_next, has_before = e < energies - 1, e > 0

    for c in range(RELAYS):
        pl.when(has_right)(lambda: to_right(k, c).start())
        pl.when(has_left)(lambda: to_left(k, c).start())

    def weights(q):
        w0, w1 = jnp.float32(0), jnp.float32(0)
        for branch in range(weight.shape[0]):
            value = weight[branch, k, q]
            w0 += jnp.where(mode[branch] == 0, 2.0 * value, 0.0)
            w1 += jnp.where(mode[branch] == 0, 0.0, value)
        return w0, w1

    own0, own1 = weights(k)
    for c in range(RELAYS):
        block = packed[k, part_of[c]].astype(F32)
        sum0[part_of[c]] = own0 * block
        sum1[part_of[c]] = own1 * block

    def take(q, c):
        w0, w1 = weights(q)
        block = packed[q, part_of[c]].astype(F32)
        sum1[part_of[c]] += w1 * block
        sum0[part_of[c]] += w0 * block

    for step in range(1, momenta):
        low, high = k - step, k + step
        for c in range(RELAYS):

            @pl.when(low >= 0)
            def _():
                q = lax.max(low, 0)
                to_right(q, c).wait_recv()
                pl.when(has_right)(lambda: to_right(q, c).start())

            @pl.when(high < momenta)
            def _():
                q = lax.min(high, momenta - 1)
                to_left(q, c).wait_recv()
                pl.when(has_left)(lambda: to_left(q, c).start())

            pl.when(low >= 0)(lambda: take(lax.max(low, 0), c))
            pl.when(high < momenta)(lambda: take(lax.min(high, momenta - 1), c))
            if step == momenta - 1:
                pl.when(has_next)(lambda: near_copy(0, c).start())
                pl.when(has_before)(lambda: near_copy(1, c).start())
    if momenta == 1:
        for c in range(RELAYS):
            pl.when(has_next)(lambda: near_copy(0, c).start())
            pl.when(has_before)(lambda: near_copy(1, c).start())

    for c in range(RELAYS):

        @pl.when(has_before)
        def _():
            near_copy(0, c).wait_recv()
            sum0[part_of[c]] += near[0, part_of[c]]

        @pl.when(has_next)
        def _():
            near_copy(1, c).wait_recv()
            sum0[part_of[c]] += near[1, part_of[c]]

    total = sum0[...]
    turned = total.T
    out_ref[:nb, :] = jnp.where(
        col > row, total, jnp.where(col < row, -turned, 0.0)
    ).astype(BF16)
    out_ref[nb:, :] = jnp.where(row >= col, total, turned).astype(BF16)
    store_self = pltpu.make_async_copy(out_ref, self_hbm, out_sem.at[1])
    store_self.start()

    for level in range(levels):
        half, sender, receiver, with_q = roles(level)

        @pl.when(sender)
        def _():
            for to in range(half):
                for c in range(CHUNKS):
                    a_copy(level, to, c).wait_send()

            @pl.when(with_q)
            def _():
                for to in range(half):
                    q_copy(level, to).wait_send()

    for c in range(RELAYS):
        for q in range(momenta):
            pl.when(jnp.logical_and(has_right, q <= k))(
                lambda: to_right(q, c).wait_send()
            )
            pl.when(jnp.logical_and(has_left, q >= k))(lambda: to_left(q, c).wait_send())
        pl.when(has_next)(lambda: near_copy(0, c).wait_send())
        pl.when(has_before)(lambda: near_copy(1, c).wait_send())
    store_green.wait()
    store_self.wait()


def on_device(free_green, coupling, coupling_tiles, occupation, phonon_weight, phonon_mode):
    slabs = lax.axis_size("slab")
    momenta = lax.axis_size("kmom")
    energies = lax.axis_size("energy")
    nb = coupling.shape[-1]
    levels = max((slabs - 1).bit_length(), 1)
    most = 1 << (levels - 1)
    hbm = pl.BlockSpec(memory_space=pl.ANY)
    dma = pltpu.SemaphoreType.DMA
    green, self_energy = pl.pallas_call(
        functools.partial(kernel, (slabs, momenta, energies, levels)),
        out_shape=(
            jax.ShapeDtypeStruct((2 * nb, nb), F32),
            jax.ShapeDtypeStruct((2 * nb, nb), BF16),
        ),
        in_specs=[hbm] * 6,
        out_specs=(hbm, hbm),
        scratch_shapes=[
            pltpu.SMEM(coupling_tiles.shape[2:] + coupling_tiles.shape[:2], jnp.int32),
            pltpu.SMEM(occupation.shape, F32),
            pltpu.SMEM(phonon_weight.shape, F32),
            pltpu.SMEM(phonon_mode.shape, jnp.int32),
            pltpu.VMEM((2 * nb, nb), F32),
            pltpu.VMEM((nb, nb), F32),
            pltpu.VMEM((2 * nb, nb), BF16),
            pltpu.VMEM((2 * nb, nb), BF16),
            pltpu.VMEM((nb, 2 * nb), BF16),
            pltpu.VMEM((nb, 2 * nb), BF16),
            pltpu.VMEM((nb, 2 * nb), BF16),
            pltpu.VMEM((nb, 2 * nb), BF16),
            pltpu.VMEM((levels, nb, 2 * nb), BF16),
            pltpu.VMEM((levels, nb, 2 * nb), BF16),
            pltpu.VMEM((momenta, nb, nb), BF16),
            pltpu.VMEM((nb, nb), F32),
            pltpu.VMEM((nb, nb), F32),
            pltpu.VMEM((2, nb, nb), F32),
            pltpu.VMEM((2 * nb, nb), BF16),
            dma((6,)),
            dma((2,)),
            dma((most, CHUNKS)),
            dma((most,)),
            dma((levels, CHUNKS)),
            dma((levels,)),
            dma((momenta, RELAYS)),
            dma((momenta, RELAYS)),
            dma((momenta, RELAYS)),
            dma((2, RELAYS)),
            dma((2, RELAYS)),
        ],
        compiler_params=pltpu.CompilerParams(
            collective_id=0, has_side_effects=True, vmem_limit_bytes=VMEM_BYTES
        ),
    )(
        free_green.reshape(2 * nb, nb),
        coupling.reshape(nb, nb),
        jnp.transpose(coupling_tiles, (2, 0, 1)),
        occupation,
        phonon_weight,
        phonon_mode,
    )
    return green.reshape(free_green.shape), self_energy.reshape(free_green.shape)


def solution(mesh):
    in_specs = (
        P("slab", "energy", "kmom", None, None, None),
        P("slab", None, None),
        P("slab", None, None),
        P("energy"),
        P(),
        P(),
    )
    out_specs = (
        P("slab", "energy", "kmom", None, None, None),
        P("slab", "energy", "kmom", None, None, None),
    )
    return jax.shard_map(
        on_device, mesh=mesh, in_specs=in_specs, out_specs=out_specs, check_vma=False
    )
```
